32 devices in a mesh: ctx: 4 (over x, core), head: 8 (over z, y).
Axes of the slice: x: 2, y: 2, z: 4, core: 2. Of those that a mesh axis runs over, the one named last changes fastest.
Arguments:
- q_latent: bfloat16 [512, 128, 576], P(('ctx', 'head')), may hold values from -84 to 84
- index_query: bfloat16 [512, 64, 128], P('head'), may hold values from -6 to 6
- index_weight: float32 [512, 64], P('head'), may hold values from -0.75 to 0.75
- index_keys: bfloat16 [8192, 128], P('ctx'), may hold values from -6 to 6
- latent_cache: bfloat16 [8192, 576], P('ctx'), may hold values from -6 to 6
- block_ids: int32 [4, 32], replicated, may hold values from 0 to 127, as said below
- block_counts: int32 [4], replicated, may hold values from 24 to 32, as said below
Outputs:
- attention: bfloat16 [512, 128, 512], P('ctx', 'head')
- index_scores: float32 [512, 8192], P('head', 'ctx')
The draws below stay inside these ranges and needn't reach their ends.
Inputs may be any that keep to these rules, and one draw needn't show every extreme that they name: `block_ids`: row t is query tile t's list of blocks of 64 positions. Its first block_counts[t] entries are distinct, lie at or before the tile's own last block and include the 2 blocks that hold the tile's own queries; of these counted entries at most 8 lie in one context shard of 32 blocks, and exactly 8 lie in the shard of the newest positions. Entries after the count are arbitrary block ids. `block_counts`: some tile has all 32 entries counted.
All inputs are finite; a program needn't handle non-finite values.
Results may differ from the reference program's by a relative error of at most 0.0034.
Values may be sent and summed in bfloat16 or wider, within the bound.
A program may use at most 128 MiB of HBM per device.

```python
import jax
import jax.numpy as jnp
from jax import lax

HEADS = 128
LATENT = 512
ROPE = 64
IDX_HEADS = 64
IDX_DIM = 128
BLOCK = 64
TILE = 128
NSEL = 32
CAP = 8
KEYS_DEV = 2048
TILES = 4
QUERIES = 512
CONTEXT = 8192


def base_cache(key):
    return jax.random.truncated_normal(jax.random.fold_in(key, 3), -6.0, 6.0, (CONTEXT, LATENT + ROPE), jnp.float32)


def draw_latent_cache(key, part):
    return base_cache(key).astype(jnp.bfloat16)


def draw_q_latent(key, part):
    base_draw = 1.5 * jax.random.truncated_normal(jax.random.fold_in(key, 5), -6.0, 6.0, (QUERIES, HEADS, LATENT + ROPE), jnp.float32)
    return base_draw.astype(jnp.bfloat16)


def block_plan(key):
    plan_keys = jax.random.split(jax.random.fold_in(key, 11), 7)
    blocks_dev = KEYS_DEV // BLOCK
    span_blocks = TILE // BLOCK
    first_new = CONTEXT // BLOCK - TILES * span_blocks
    last_start = CONTEXT // BLOCK - blocks_dev
    counts = jax.random.randint(plan_keys[0], (TILES,), NSEL - NSEL // 4, NSEL + 1)
    full_tile = jax.random.randint(plan_keys[1], (), 0, TILES)
    tile_range = jnp.arange(TILES)
    counts = jnp.where(tile_range == full_tile, NSEL, counts)
    local_index = jnp.arange(blocks_dev)
    limit_local = first_new - last_start + tile_range * span_blocks
    rand_last = jax.random.randint(plan_keys[2], (TILES, blocks_dev), 0, 1 << 20)
    score_last = jnp.where(local_index[None, :] < limit_local[:, None], rand_last, (1 << 20) + local_index[None, :]) * blocks_dev + local_index[None, :]
    pick_last = jnp.argsort(score_last, axis=1)[:, :CAP - span_blocks] + last_start
    diagonal_blocks = first_new + tile_range[:, None] * span_blocks + jnp.arange(span_blocks)[None, :]
    others = TILES - 1
    rand_other = jax.random.randint(plan_keys[3], (TILES, others, blocks_dev), 0, 1 << 20) * blocks_dev + local_index[None, None, :]
    pick_other = jnp.argsort(rand_other, axis=2)[:, :, :CAP] + (jnp.arange(others) * blocks_dev)[None, :, None]
    pool_blocks = pick_other.reshape(TILES, others * CAP)
    rand_pool = jax.random.randint(plan_keys[4], (TILES, others * CAP), 0, 1 << 20) * (others * CAP) + jnp.arange(others * CAP)[None, :]
    pool_blocks = jnp.take_along_axis(pool_blocks, jnp.argsort(rand_pool, axis=1), axis=1)[:, :NSEL - CAP]
    ordered = jnp.concatenate([diagonal_blocks, pick_last, pool_blocks], axis=1)
    entry_index = jnp.arange(NSEL)
    rand_valid = jax.random.randint(plan_keys[5], (TILES, NSEL), 0, 1 << 20) * NSEL + entry_index[None, :]
    order_score = jnp.where(entry_index[None, :] < counts[:, None], rand_valid, ((1 << 20) + 1) * NSEL + entry_index[None, :])
    shuffled = jnp.take_along_axis(ordered, jnp.argsort(order_score, axis=1), axis=1)
    filler = jax.random.randint(plan_keys[6], (TILES, NSEL), 0, CONTEXT // BLOCK)
    listed = jnp.where(entry_index[None, :] < counts[:, None], shuffled, filler)
    return (listed.astype(jnp.int32), counts.astype(jnp.int32))


def draw_block_ids(key, part):
    listed, counts = block_plan(key)
    return listed


def draw_block_counts(key, part):
    listed, counts = block_plan(key)
    return counts


def shard_levels(stream_key, extent, shards, low, top_value):
    def one(position, blocks):
        steps = jax.random.uniform(jax.random.fold_in(jax.random.fold_in(stream_key, 6), position), (blocks,), jnp.float32, low / len(shards), top_value / len(shards))
        return jnp.repeat(jnp.exp(steps), extent[position] // blocks).reshape((-1,) + (1,) * (len(extent) - position - 1))

    factor_of = one(*shards[0])
    for cut in shards[1:]:
        factor_of = factor_of * one(*cut)
    return factor_of


def gaussian(stream_key, extent, spread, limit, pieces=(), kind=jnp.bfloat16):
    entries = jax.random.normal(stream_key, extent, jnp.float32) * spread
    if len(pieces) > 0:
        entries = shard_levels(stream_key, extent, pieces, -0.22, 0.18) * entries
    return jnp.clip(entries, min=-limit, max=limit).astype(kind)


def setup_inputs(seed: int = 0) -> dict:
    arg_keys = jax.random.split(jax.random.key(seed), 8)
    return {
        "q_latent": draw_q_latent(jax.random.fold_in(arg_keys[7], 71), 0),
        "index_query": gaussian(arg_keys[1], (QUERIES, IDX_HEADS, IDX_DIM), 1.0, 6.0, ((0, 8),)),
        "index_weight": gaussian(arg_keys[2], (QUERIES, IDX_HEADS), IDX_HEADS ** -0.5, 0.75, ((0, 8),), jnp.float32),
        "index_keys": gaussian(arg_keys[3], (CONTEXT, IDX_DIM), 1.0, 6.0, ((0, 4),)),
        "latent_cache": draw_latent_cache(jax.random.fold_in(arg_keys[7], 71), 0),
        "block_ids": draw_block_ids(jax.random.fold_in(arg_keys[7], 71), 0),
        "block_counts": draw_block_counts(jax.random.fold_in(arg_keys[7], 71), 0),
    }


softmax_scale = 192.0 ** -0.5


def index_block(index_query, index_weight, key_block):
    flat_query = index_query.reshape(-1, index_query.shape[2])
    raw_dots = lax.dot_general(flat_query, key_block, (((1,), (1,)), ((), ())), preferred_element_type=jnp.float32)
    gated_dots = jax.nn.relu(raw_dots * index_query.shape[2] ** -0.5).reshape(index_query.shape[0], index_query.shape[1], -1)
    return jnp.sum(gated_dots * index_weight[:, :, None], axis=1)


def attend_rows(query_block, key_rows, allowed):
    rows_here = query_block.shape[0]
    heads_here = query_block.shape[1]
    flat_query = query_block.reshape(rows_here * heads_here, -1)
    raw_scores = lax.dot_general(flat_query, key_rows, (((1,), (1,)), ((), ())), preferred_element_type=jnp.float32)
    raw_scores = raw_scores.reshape(rows_here, heads_here, -1) * softmax_scale
    masked = jnp.where(allowed[:, None, :], raw_scores, -jnp.inf)
    row_max = jnp.max(masked, axis=2, keepdims=True)
    exp_scores = jnp.exp(masked - row_max)
    totals = jnp.sum(exp_scores, axis=2, keepdims=True)
    weights = exp_scores.astype(jnp.bfloat16).reshape(rows_here * heads_here, -1)
    weighted_sum = jnp.dot(weights, key_rows[:, :LATENT], preferred_element_type=jnp.float32)
    return (weighted_sum.reshape(rows_here, heads_here, LATENT) / totals).astype(jnp.bfloat16)


def reference(q_latent, index_query, index_weight, index_keys, latent_cache, block_ids, block_counts):
    context = latent_cache.shape[0]
    queries = q_latent.shape[0]
    key_span = 8 * BLOCK
    key_blocks = index_keys.reshape(context // key_span, key_span, IDX_DIM)
    per_block = lax.map(lambda key_block: index_block(index_query, index_weight, key_block), key_blocks)
    index_scores = jnp.transpose(per_block, (1, 0, 2)).reshape(queries, context)

    def one_tile(tile_index):
        tile_blocks = block_ids[tile_index]
        entry_index = jnp.arange(NSEL, dtype=jnp.int32)
        tile_live = entry_index < block_counts[tile_index]
        key_pos = (tile_blocks[:, None] * BLOCK + jnp.arange(BLOCK, dtype=jnp.int32)[None, :]).reshape(-1)
        key_live = jnp.repeat(tile_live, BLOCK)
        key_rows = jnp.take(latent_cache, key_pos, axis=0)
        query_pos = (context - queries) + tile_index * TILE + jnp.arange(TILE, dtype=jnp.int32)
        allowed = key_live[None, :] & (key_pos[None, :] <= query_pos[:, None])
        tile_query = lax.dynamic_slice_in_dim(q_latent, (tile_index * TILE).astype(jnp.int32), TILE, 0)
        return attend_rows(tile_query, key_rows, allowed)

    per_tile = lax.map(one_tile, jnp.arange(TILES, dtype=jnp.int32))
    attention = per_tile.reshape(queries, HEADS, LATENT)
    return attention, index_scores
```

```python
import functools

import jax
import jax.numpy as jnp
from jax import lax
from jax.experimental import pallas as pl
from jax.experimental.pallas import tpu as pltpu
from jax.sharding import PartitionSpec as P

ROPE = 64
BLOCK = 64
CAP = 8
LANES = 128
FAR = 1 << 28

softmax_scale = 192.0 ** (-0.5)


def flip(index, mask, bits):
    total = 0
    for b in range(bits):
        w = 1 << b
        total = total + lax.rem(lax.div(index, w) + (mask // w) % 2, 2) * w
    return total


def kernel(
    C, H,
    q_hbm, iq_hbm, iw_hbm, ik_hbm, cache_hbm, ids, counts,
    att_hbm, idx_hbm,
    q_v, iq_v, iw_v, ik_v, cache_v, stage, recv, ksend, krecv, kpos, wcol, obuf, ibuf,
    in_sem, qs_sem, qr_sem, ks_sem, kr_sem, own_sem, out_sem, idx_sem,
):
    ctx = lax.axis_index("ctx")
    head = lax.axis_index("head")
    nq, heads, feat = q_v.shape
    lat = feat - ROPE
    hs = heads // H
    rows = nq * hs
    half = rows // 2
    lat_tiles = lat // LANES
    blocks_dev = cache_v.shape[0]
    keys_dev = blocks_dev * BLOCK
    nsel = ids.shape[1]
    tile = nq * H
    span = CAP * BLOCK
    keys = C * span
    bits = H.bit_length() - 1

    loads = [
        pltpu.make_async_copy(q_hbm, q_v, in_sem.at[0]),
        pltpu.make_async_copy(cache_hbm, cache_v, in_sem.at[1]),
        pltpu.make_async_copy(iw_hbm, iw_v, in_sem.at[2]),
        pltpu.make_async_copy(iq_hbm, iq_v, in_sem.at[3]),
        pltpu.make_async_copy(ik_hbm, ik_v, in_sem.at[4]),
    ]
    for copy in loads:
        copy.start()

    barrier = pltpu.get_barrier_semaphore()
    for k in range(1, H):
        pl.semaphore_signal(barrier, inc=1, device_id={"head": flip(head, k, bits)},
                            device_id_type=pl.DeviceIdType.MESH)
    for k in range(1, C):
        pl.semaphore_signal(barrier, inc=1, device_id={"ctx": lax.rem(ctx + k, C)},
                            device_id_type=pl.DeviceIdType.MESH)

    loads[0].wait()
    for p in range(H):
        piece = q_v[:, p * hs:(p + 1) * hs, :].astype(jnp.float32).reshape(rows, feat)
        for t in range(lat_tiles):
            stage[p, t * rows:(t + 1) * rows, :] = piece[:, t * LANES:(t + 1) * LANES].astype(jnp.bfloat16)
        rope = piece[:, lat:]
        stage[p, lat_tiles * rows:, :] = jnp.concatenate([rope[:half], rope[half:]], axis=1).astype(jnp.bfloat16)

    pl.semaphore_wait(barrier, H - 1 + C - 1)

    order = list(range(H - 1, 0, -1))

    def q_copy(k):
        peer = flip(head, k, bits)
        return pltpu.make_async_remote_copy(
            src_ref=stage.at[peer], dst_ref=recv.at[head],
            send_sem=qs_sem.at[k - 1], recv_sem=qr_sem.at[k - 1],
            device_id={"head": peer}, device_id_type=pl.DeviceIdType.MESH)

    for k in order:
        q_copy(k).start()

    def slots(tile_index, shard):
        count = counts[tile_index]

        n = jnp.int32(0)
        table = [jnp.int32(-1)] * CAP
        for e in range(nsel):
            block = ids[tile_index, e]
            mine = jnp.logical_and(e < count, lax.div(block, blocks_dev) == shard)
            local = lax.rem(block, blocks_dev)
            table = [
                jnp.where(jnp.logical_and(mine, n == s), local, old) for s, old in enumerate(table)
            ]
            n = n + mine.astype(jnp.int32)
        return table

    loads[1].wait()

    def k_copy(d):
        to = lax.rem(ctx + d, C)
        return pltpu.make_async_remote_copy(
            src_ref=ksend.at[to], dst_ref=krecv.at[ctx],
            send_sem=ks_sem.at[d - 1], recv_sem=kr_sem.at[d - 1],
            device_id={"ctx": to}, device_id_type=pl.DeviceIdType.MESH)

    pad = jnp.zeros((BLOCK, LANES - ROPE), jnp.bfloat16)
    near = [d for d in range(1, C)]
    for d in near + [0]:
        to = lax.rem(ctx + d, C)
        for s, local in enumerate(slots(to, ctx)):
            part = cache_v[jnp.maximum(local, 0)]
            ksend[to, s * BLOCK:(s + 1) * BLOCK, :lat] = part[:, :lat]
            ksend[to, s * BLOCK:(s + 1) * BLOCK, lat:] = jnp.concatenate([part[:, lat:], pad], axis=1)
        if d:
            k_copy(d).start()
    own = pltpu.make_async_copy(ksend.at[ctx], krecv.at[ctx], own_sem)
    own.start()

    lane = lax.broadcasted_iota(jnp.int32, (1, LANES), 1)
    per = LANES // BLOCK
    for shard in range(C):
        table = slots(ctx, jnp.int32(shard))
        bases = [
            jnp.where(local < 0, FAR, (shard * blocks_dev + local) * BLOCK) for local in table
        ]
        for j in range(CAP // per):
            low, high = bases[j * per], bases[j * per + 1]
            kpos[0:1, shard * span + j * LANES:shard * span + (j + 1) * LANES] = jnp.where(
                lane < BLOCK, low + lane, high + (lane - BLOCK))

    iqn, ih, idim = iq_hbm.shape
    for n in (2, 3, 4):
        loads[n].wait()
    w_t = (iw_v[...] * (idim ** -0.5)).T
    for i in range(iqn):
        wcol[i] = jnp.broadcast_to(w_t[:, i:i + 1], (ih, LANES))
    group = 8
    wide = 256

    def index_step(g, _):
        qs = iq_v[pl.ds(g * group, group)].reshape(group * ih, idim)
        w = wcol[pl.ds(g * group, group)]
        for j in range(keys_dev // wide):
            dots = lax.dot_general(
                qs, ik_v[j * wide:(j + 1) * wide, :], (((1,), (1,)), ((), ())),
                preferred_element_type=jnp.float32)
            gated = jnp.maximum(dots, 0.0).reshape(group, ih, wide)
            for u in range(wide // LANES):
                ibuf[pl.ds(pl.multiple_of(g * group, group), group), j * wide + u * LANES:j * wide + (u + 1) * LANES] = jnp.sum(
                    gated[:, :, u * LANES:(u + 1) * LANES] * w, axis=1)
        return 0

    lax.fori_loop(0, iqn // group, index_step, 0)
    idx_out = pltpu.make_async_copy(ibuf, idx_hbm, idx_sem)
    idx_out.start()

    own.wait()
    for d in near:
        k_copy(d).wait_send()
        source = lax.rem(ctx - d + C, C)
        pltpu.make_async_remote_copy(
            src_ref=ksend.at[source], dst_ref=krecv.at[source],
            send_sem=ks_sem.at[d - 1], recv_sem=kr_sem.at[d - 1],
            device_id={"ctx": source}, device_id_type=pl.DeviceIdType.MESH).wait_recv()

    def attend(chunk_ref, source):
        parts = [chunk_ref[t * rows:(t + 1) * rows, :] for t in range(lat_tiles)]
        pair = chunk_ref[lat_tiles * rows:, :].astype(jnp.float32)
        turned = jnp.concatenate([pair[:, ROPE:], pair[:, :ROPE]], axis=1)
        rope = jnp.concatenate([pair, turned], axis=0).astype(jnp.bfloat16)
        lhs = jnp.concatenate(parts + [rope], axis=1)
        key_rows = krecv[...].reshape(keys, lat + LANES)
        scores = lax.dot_general(
            lhs, key_rows, (((1,), (1,)), ((), ())), preferred_element_type=jnp.float32
        ) * softmax_scale
        first = C * (keys_dev - tile) + ctx * tile + source * nq
        qpos = first + lax.broadcasted_iota(jnp.int32, (rows, 1), 0) // hs
        scores = jnp.where(kpos[...] <= qpos, scores, -jnp.inf)
        top = jnp.max(scores, axis=1, keepdims=True)
        expd = jnp.exp(scores - top)
        total = jnp.sum(expd, axis=1, keepdims=True)
        out = jnp.dot(expd.astype(jnp.bfloat16), key_rows[:, :lat], preferred_element_type=jnp.float32)
        out = out * (1.0 / total)
        obuf[source] = out.reshape(nq, hs, lat).astype(jnp.bfloat16)

    def out_copy(source):
        return pltpu.make_async_copy(
            obuf.at[source], att_hbm.at[pl.ds(source * nq, nq)], out_sem.at[source])

    attend(stage.at[head], head)
    out_copy(head).start()

    def peer_step(i, _):
        k = H - 1 - i
        peer = flip(head, k, bits)
        pltpu.make_async_remote_copy(
            src_ref=stage.at[peer], dst_ref=recv.at[peer],
            send_sem=qs_sem.at[k - 1], recv_sem=qr_sem.at[k - 1],
            device_id={"head": peer}, device_id_type=pl.DeviceIdType.MESH).wait()
        attend(recv.at[peer], peer)
        out_copy(peer).start()
        return 0

    lax.fori_loop(0, H - 1, peer_step, 0)
    for source in range(H):
        out_copy(source).wait()
    idx_out.wait()


def body(q_latent, index_query, index_weight, index_keys, latent_cache, block_ids, block_counts):
    C = lax.axis_size("ctx")
    H = lax.axis_size("head")
    nq, heads, feat = q_latent.shape
    lat = feat - ROPE
    hs = heads // H
    rows = nq * hs
    keys_dev = latent_cache.shape[0]
    span = CAP * BLOCK
    packed = rows * (lat // LANES) + rows // 2
    iqn, ih, idim = index_query.shape
    any_spec = pl.BlockSpec(memory_space=pl.ANY)
    smem = pl.BlockSpec(memory_space=pltpu.SMEM)
    bf16, f32 = jnp.bfloat16, jnp.float32
    dma = pltpu.SemaphoreType.DMA
    return pl.pallas_call(
        functools.partial(kernel, C, H),
        out_shape=(
            jax.ShapeDtypeStruct((nq * H, hs, lat), bf16),
            jax.ShapeDtypeStruct((iqn, keys_dev), f32),
        ),
        in_specs=[any_spec] * 5 + [smem] * 2,
        out_specs=(any_spec, any_spec),
        scratch_shapes=[
            pltpu.VMEM((nq, heads, feat), bf16),
            pltpu.VMEM((iqn, ih, idim), bf16),
            pltpu.VMEM((iqn, ih), f32),
            pltpu.VMEM((keys_dev, idim), bf16),
            pltpu.VMEM((keys_dev // BLOCK, BLOCK, feat), bf16),
            pltpu.VMEM((H, packed, LANES), bf16),
            pltpu.VMEM((H, packed, LANES), bf16),
            pltpu.VMEM((C, span, lat + LANES), bf16),
            pltpu.VMEM((C, span, lat + LANES), bf16),
            pltpu.VMEM((1, C * span), jnp.int32),
            pltpu.VMEM((iqn, ih, LANES), f32),
            pltpu.VMEM((H, nq, hs, lat), bf16),
            pltpu.VMEM((iqn, keys_dev), f32),
            dma((5,)),
            dma((H - 1,)),
            dma((H - 1,)),
            dma((C - 1,)),
            dma((C - 1,)),
            dma(()),
            dma((H,)),
            dma(()),
        ],
        compiler_params=pltpu.CompilerParams(
            collective_id=0, has_side_effects=True, vmem_limit_bytes=56 * 1024 * 1024
        ),
        cost_estimate=pl.CostEstimate(flops=12_000_000_000, bytes_accessed=12_000_000, transcendentals=4_000_000),
    )(q_latent, index_query, index_weight, index_keys, latent_cache.reshape(keys_dev // BLOCK, BLOCK, feat),
      block_ids, block_counts)


def solution(mesh):
    return jax.shard_map(
        body,
        mesh=mesh,
        in_specs=(
            P(("ctx", "head"), None, None),
            P("head", None, None),
            P("head", None),
            P("ctx", None),
            P("ctx", None),
            P(),
            P(),
        ),
        out_specs=(P("ctx", "head", None), P("head", "ctx")),
        check_vma=False,
    )
```
